32 devices in a mesh: seq: 8 (over y, x, core), exp: 4 (over z).
Axes of the slice: x: 2, y: 2, z: 4, core: 2. Of those that a mesh axis runs over, the one named last changes fastest.
Arguments:
- mixer_input: bfloat16 [512, 8192], P('seq', 'exp'), may hold values from -6 to 6
- gate_input: bfloat16 [512, 8192], P('seq', 'exp'), may hold values from -6 to 6
- delta_raw: bfloat16 [512, 8192], P('seq', 'exp'), may hold values from -7 to 2051
- input_coef: bfloat16 [512, 16], P('seq'), may hold values from 0.19921875 to 1.796875
- output_coef: bfloat16 [512, 16], P('seq'), may hold values from -3 to 3
- decay_rate: float32 [16, 8192], P(None, 'exp'), may hold values from 3.90625e-05 to 0.05
- conv_weight: float32 [4, 8192], P(None, 'exp'), may hold values from -3 to 3
- conv_bias: float32 [8192], P('exp'), may hold values from -3 to 3
- skip_gain: float32 [8192], P('exp'), may hold values from 0.5 to 1.5
- out_weight: bfloat16 [8192, 4096], P('exp', 'seq'), may hold values from -0.0625 to 0.0625
- residual: bfloat16 [512, 4096], P(('seq', 'exp')), may hold values from -6 to 6
- norm_gain: float32 [4096], replicated, may hold values from 0.1 to 1.9
- router_weight: bfloat16 [4096, 4], replicated, may hold values from -0.09375 to 0.09375
- expert_ids: int32 [512, 2], P(('seq', 'exp')), may hold values from 0 to 3, all different within a row; in each aligned block of 16 rows (0 to 15, 16 to 31, ...) at most 9 rows name the same one
- gate_weight: bfloat16 [4, 4096, 12288], P('exp', None, 'seq'), may hold values from -0.09375 to 0.09375
- up_weight: bfloat16 [4, 4096, 12288], P('exp', None, 'seq'), may hold values from -0.09375 to 0.09375
- down_weight: bfloat16 [4, 12288, 4096], P('exp', 'seq'), may hold values from -0.0546875 to 0.0546875
Outputs:
- mixed: bfloat16 [512, 8192], P('seq', 'exp')
- final: bfloat16 [512, 4096], P(('seq', 'exp'))
The draws below stay inside these ranges and needn't reach their ends.
Inputs may be any that keep to these rules, and one draw needn't show every extreme that they name: `expert_ids`: each row names two different experts. In each aligned block of 16 rows (the rows of one device) no expert is named by more than 9 rows, and in some block one expert is named by exactly 9 rows.
All inputs are finite; a program needn't handle non-finite values.
Results may differ from the reference program's by a relative error of at most 0.015.
Values may be sent and summed in bfloat16 or wider, within the bound.
A program may use at most 128 MiB of HBM per device.

```python
import math
import jax
import jax.numpy as jnp
import numpy as np
from jax import lax

D = 4096
INNER = 8192
STATE = 16
KCONV = 4
FF = 12288
ROWS = 16
EXPERTS = 4
SEQ = 512
CAP = 9
N_SEQ = 8
N_EXP = 4


def draw_delta_raw(key, part):
    base_key = jax.random.fold_in(key, 11)
    spot_key = jax.random.fold_in(key, 12)
    height_key = jax.random.fold_in(key, 13)
    base = jnp.clip(jax.random.normal(base_key, (SEQ, INNER), jnp.float32) - 0.5, -6.5, 3.0)
    spots = jax.random.randint(spot_key, (3,), 0, SEQ)
    heights = jax.random.uniform(height_key, (3,), jnp.float32, 0.5, 2.0) * SEQ
    hits = jnp.arange(SEQ)[:, None] == spots[None, :]
    boost = jnp.sum(jnp.where(hits, heights[None, :], 0.0), axis=1)
    return (base + boost[:, None]).astype(jnp.bfloat16)


def draw_decay_rate(key, part):
    lowest = jnp.float32(0.02) / SEQ
    low = jnp.log(lowest)
    high = jnp.log(jnp.float32(0.05))
    spread_key = jax.random.fold_in(key, 21)
    logs = jax.random.uniform(spread_key, (STATE, INNER), jnp.float32) * (high - low) + low
    return jnp.clip(jnp.exp(logs), lowest, jnp.float32(0.05))


def level_of(key, extent, shards, low, top_value):
    loudness = 1.0
    for dim, shards_of in shards:
        draws = jax.random.uniform(jax.random.fold_in(jax.random.fold_in(key, 6), dim), (shards_of,), jnp.float32, low / len(shards), top_value / len(shards))
        loudness = loudness * jnp.repeat(jnp.exp(draws), extent[dim] // shards_of).reshape((-1,) + (1,) * (len(extent) - 1 - dim))
    return loudness


def shared_out(rng, own, number, rows, count, top, limit, slope):
    order = jax.random.permutation(rng, count)
    heavy_load, common = load_shares(count, rows * top, limit, slope, True), load_shares(count, rows * top, limit, slope, False)
    places = jnp.arange(count)

    def named(lengths, offset_by):
        used = int((lengths > 0).sum())
        fixed = max(1, used // 4)
        moved = fixed + (places - fixed + offset_by * (used - fixed)) % max(1, count - fixed)
        return jnp.zeros((count,), jnp.int32).at[order[jnp.where(places < fixed, places, moved)]].set(jnp.asarray(lengths, jnp.int32))

    lengths = jnp.where(number % 4 == 0, named(heavy_load, number // 4), named(common, number - number // 4 - 1))
    mixed = jax.random.permutation(jax.random.fold_in(own, 3), count)
    donor, taker = mixed[0:count // 2 * 2:2], mixed[1:count // 2 * 2:2]
    margin = jnp.minimum(lengths[donor] - 1, limit - lengths[taker]) // 2
    margin = jnp.where((donor == order[0]) | (taker == order[0]) | (lengths[taker] == 0), 0, jnp.maximum(margin, 0))
    moved = jax.random.randint(jax.random.fold_in(own, 4), (count // 2,), 0, 1 << 20) % (margin + 1)
    lengths = lengths.at[donor].add(-moved).at[taker].add(moved)
    members = jnp.searchsorted(jnp.cumsum(lengths), jnp.arange(rows * top), side="right").astype(jnp.int32)
    grid = members.reshape(top, rows).T
    grid = grid[jax.random.permutation(jax.random.fold_in(own, 1), rows)]
    offset_by = jax.random.randint(jax.random.fold_in(own, 2), (rows, 1), 0, top)
    return jnp.take_along_axis(grid, (jnp.arange(top)[None, :] + offset_by) % top, axis=1)


def load_shares(amount, total, reach, lean, full):
    loads = [(1 << 20) // math.isqrt(rank ** lean) + 1 for rank in range(1, amount + 1)]
    largest = reach if full else min(reach, max(-(-total // amount), total * loads[0] // sum(loads)))
    least = 1 if total - largest >= amount - 1 else 0
    counts, spare = [largest] + [least] * (amount - 1), total - largest - least * (amount - 1)
    while spare > 0:
        free = [i for i in range(1, amount) if counts[i] < largest] or [i for i in range(1, amount) if counts[i] < reach]
        pool, budget = sum([loads[i] for i in free]), spare
        for i in free:
            extra = min(reach - counts[i], max(1, budget * loads[i] // pool), spare)
            counts[i] = counts[i] + extra
            spare = spare - extra
    return np.array(counts)


def gaussian(stream_key, dims, spread, limit, split=(), kind=jnp.bfloat16):
    values = spread * jax.random.normal(stream_key, dims, jnp.float32)
    if split:
        values = values * level_of(stream_key, dims, split, -0.22, 0.18)
    return jnp.clip(values, -limit, limit).astype(kind)


def setup_inputs(seed: int = 0) -> dict:
    arg_keys = jax.random.split(jax.random.key(seed), 18)
    mixer_input = gaussian(arg_keys[0], (SEQ, INNER), 1.0, 6.0, ((0, 8), (1, 4)))
    gate_input = gaussian(arg_keys[1], (SEQ, INNER), 1.0, 6.0, ((0, 8), (1, 4)))
    delta_raw = draw_delta_raw(jax.random.fold_in(arg_keys[17], 71), 0)
    input_coef = jnp.clip(0.19921875 + 1.5976562 * jax.random.uniform(arg_keys[3], (SEQ, STATE), jnp.float32) ** level_of(arg_keys[3], (SEQ, STATE), ((0, 8),), -0.2, 0.2), 0.19921875, 1.796875).astype(jnp.bfloat16)
    output_coef = gaussian(arg_keys[4], (SEQ, STATE), 0.5, 3.0, ((0, 8),))
    decay_rate = draw_decay_rate(jax.random.fold_in(arg_keys[17], 71), 0)
    conv_weight = gaussian(arg_keys[6], (KCONV, INNER), 0.5, 3.0, ((1, 4),), jnp.float32)
    conv_bias = gaussian(arg_keys[7], (INNER,), 0.5, 3.0, ((0, 4),), jnp.float32)
    skip_gain = jnp.clip(0.5 + 1.0 * jax.random.uniform(arg_keys[8], (INNER,), jnp.float32) ** level_of(arg_keys[8], (INNER,), ((0, 4),), -0.2, 0.2), 0.5, 1.5)
    out_weight = gaussian(arg_keys[9], (INNER, D), INNER ** -0.5, 0.0625, ((0, 4), (1, 8)))
    residual = gaussian(arg_keys[10], (SEQ, D), 1.0, 6.0, ((0, 32),))
    norm_gain = jnp.clip(1.0 + 0.18 * jax.random.normal(arg_keys[11], (D,), jnp.float32), 0.1, 1.9)
    router_weight = gaussian(arg_keys[12], (D, EXPERTS), D ** -0.5, 0.09375)
    expert_ids_keys = jax.random.split(jax.random.fold_in(arg_keys[13], 1), SEQ // ROWS)
    expert_ids_turns = jax.random.permutation(jax.random.fold_in(arg_keys[13], 3), SEQ // ROWS)
    expert_ids = jax.vmap(lambda own, number: shared_out(jax.random.fold_in(arg_keys[13], 2), own, number, ROWS, EXPERTS, 2, CAP, 2))(expert_ids_keys, expert_ids_turns).reshape((SEQ, 2))
    gate_weight = gaussian(arg_keys[14], (EXPERTS, D, FF), D ** -0.5, 0.09375, ((0, 4), (2, 8)))
    up_weight = gaussian(arg_keys[15], (EXPERTS, D, FF), D ** -0.5, 0.09375, ((0, 4), (2, 8)))
    down_weight = gaussian(arg_keys[16], (EXPERTS, FF, D), FF ** -0.5, 0.0546875, ((0, 4), (1, 8)))
    return {"mixer_input": mixer_input, "gate_input": gate_input, "delta_raw": delta_raw, "input_coef": input_coef, "output_coef": output_coef, "decay_rate": decay_rate, "conv_weight": conv_weight, "conv_bias": conv_bias, "skip_gain": skip_gain, "out_weight": out_weight, "residual": residual, "norm_gain": norm_gain, "router_weight": router_weight, "expert_ids": expert_ids, "gate_weight": gate_weight, "up_weight": up_weight, "down_weight": down_weight}


def convolve(mixer_input, conv_weight, conv_bias):
    width = mixer_input.shape[1]
    values = mixer_input.astype(jnp.float32)
    length = values.shape[0]
    padded = jnp.concatenate([jnp.zeros((KCONV - 1, width), jnp.float32), values], axis=0)
    summed = jnp.broadcast_to(conv_bias[None, :], (length, width)).astype(jnp.float32)
    for offset in range(KCONV):
        summed = summed + conv_weight[offset][None, :] * padded[offset:offset + length]
    return jax.nn.silu(summed)

def sweep(state, delta, convolved, input_rows, output_rows, decay_rate):

    def advance(carry, inputs):
        delta_row, value_row, input_row, output_row = inputs
        retain = jnp.exp(-delta_row[None, :] * decay_rate)
        carry = retain * carry + (1.0 - retain) * input_row[:, None] * value_row[None, :]
        return (carry, lax.optimization_barrier(jnp.sum(output_row[:, None] * carry, axis=0)))
    return lax.scan(advance, state, (delta, convolved, input_rows, output_rows), unroll=8)

def reference(mixer_input, gate_input, delta_raw, input_coef, output_coef, decay_rate, conv_weight, conv_bias, skip_gain, out_weight, residual, norm_gain, router_weight, expert_ids, gate_weight, up_weight, down_weight):
    convolved = convolve(mixer_input, conv_weight, conv_bias)
    delta = jax.nn.softplus(delta_raw.astype(jnp.float32))
    zero_state = jnp.zeros((STATE, INNER), jnp.float32)
    end_state, scan_out = sweep(zero_state, delta, convolved, input_coef.astype(jnp.float32), output_coef.astype(jnp.float32), decay_rate)
    mixed = ((scan_out + skip_gain[None, :] * convolved) * jax.nn.silu(gate_input.astype(jnp.float32))).astype(jnp.bfloat16)
    block = INNER // N_EXP
    projected = jnp.zeros((SEQ, D), jnp.float32)
    for owner in range(N_EXP):
        term = jnp.dot(mixed[:, owner * block:(owner + 1) * block], out_weight[owner * block:(owner + 1) * block], preferred_element_type=jnp.float32)
        projected = projected + lax.optimization_barrier(term.astype(jnp.bfloat16)).astype(jnp.float32)
    hidden_state = residual.astype(jnp.float32) + projected
    scale = lax.rsqrt(lax.optimization_barrier(jnp.mean(hidden_state * hidden_state, axis=1, keepdims=True)) + 1e-06)
    normed = (hidden_state * scale * norm_gain[None, :]).astype(jnp.bfloat16)
    logits = jnp.dot(normed, router_weight, preferred_element_type=jnp.float32)
    chosen = jnp.take_along_axis(logits, expert_ids, axis=1)
    first = jax.nn.sigmoid(chosen[:, 0] - chosen[:, 1])
    blocks = expert_ids.reshape(-1, 2 * ROWS)
    onehot = (blocks[:, :, None] == jnp.arange(EXPERTS, dtype=jnp.int32)[None, None, :]).astype(jnp.int32)
    before = (jnp.cumsum(onehot, axis=1) - onehot).astype(jnp.int32)
    rank = lax.optimization_barrier(jnp.sum(before * onehot, axis=2)).astype(jnp.int32).reshape(SEQ, 2)
    per_expert = SEQ // ROWS * CAP
    owner_block = (jnp.arange(SEQ, dtype=jnp.int32) // ROWS)[:, None]
    slot_index = (expert_ids * per_expert + owner_block * CAP + rank).astype(jnp.int32).reshape(-1)
    repeated = jnp.broadcast_to(normed[:, None, :], (SEQ, 2, D)).reshape(-1, D)
    buffer = jnp.zeros((EXPERTS * per_expert, D), jnp.bfloat16).at[slot_index].set(repeated).reshape(EXPERTS, per_expert, D)
    hidden_block = FF // N_SEQ

    def serve(operands):
        routed, gate_part, up_part, down_part = operands
        gating = jnp.dot(routed, gate_part, preferred_element_type=jnp.float32)
        upward = jnp.dot(routed, up_part, preferred_element_type=jnp.float32)
        activated = (jax.nn.silu(gating) * upward).astype(jnp.bfloat16)

        def add_block(index, total):
            begin = index * hidden_block
            portion = lax.dynamic_slice_in_dim(activated, begin, hidden_block, 1)
            weights = lax.dynamic_slice_in_dim(down_part, begin, hidden_block, 0)
            term = jnp.dot(portion, weights, preferred_element_type=jnp.float32)
            return total + lax.optimization_barrier(term.astype(jnp.bfloat16)).astype(jnp.float32)
        total = lax.fori_loop(0, N_SEQ, add_block, jnp.zeros((routed.shape[0], D), jnp.float32))
        return total.astype(jnp.bfloat16)
    expert_out = lax.map(serve, (buffer, gate_weight, up_weight, down_weight))
    returned = expert_out.reshape(-1, D)[slot_index].astype(jnp.float32).reshape(SEQ, 2, D)
    moe_out = first[:, None] * returned[:, 0] + (1.0 - first)[:, None] * returned[:, 1]
    final = (hidden_state + moe_out).astype(jnp.bfloat16)
    return (mixed, final)
```

```python
import functools

import jax
import jax.numpy as jnp
from jax import lax
from jax.experimental import pallas as pl
from jax.experimental.pallas import tpu as pltpu
from jax.sharding import PartitionSpec as P

KCONV = 4
MESH = pl.DeviceIdType.MESH
VMEM_LIMIT = 58 * 2**20


def from_behind(block, axis, distance):
    devices = range(lax.axis_size(axis))
    route = [(i - distance, i) for i in devices if i - distance in devices]
    return lax.ppermute(block, axis, route)


def place():
    me = lax.axis_index("seq")
    z = lax.axis_index("exp")
    core = lax.rem(me, 2)
    return me, z, core, lax.div(me, 2)


def greet(peers):
    barrier = pltpu.get_barrier_semaphore()
    for peer in peers:
        pl.semaphore_signal(barrier, inc=1, device_id=peer, device_id_type=MESH)
    pl.semaphore_wait(barrier, len(peers))


def push(src, dst, send_sem, recv_sem, peer):
    return pltpu.make_async_remote_copy(
        src_ref=src,
        dst_ref=dst,
        send_sem=send_sem,
        recv_sem=recv_sem,
        device_id=peer,
        device_id_type=MESH,
    )


def mixer_kernel(
    n, conv_ref, delta_ref, in_ref, out_coef_ref, rate_ref, skip_ref, gate_ref, out_ref,
    own_end, own_sum, ends, sums, start, s_end, r_end, s_sum, r_sum,
):
    me, z, core, chip = place()
    groups, states, span = own_end.shape
    parts = span // 128
    blocks = conv_ref.shape[0] // 16

    barrier = pltpu.get_barrier_semaphore()
    for d in range(1, n):
        peer = (lax.rem(me + d, n), z)
        pl.semaphore_signal(barrier, inc=1, device_id=peer, device_id_type=MESH)

    def copies(g, d):
        peer = (lax.rem(me + d, n), z)
        i = d - 1
        return (
            push(own_end.at[g], ends.at[g, i], s_end.at[g, i], r_end.at[g, i], peer),
            push(own_sum.at[g], sums.at[g, i], s_sum.at[g, i], r_sum.at[g, i], peer),
        )

    def walk(g, begin, emit):

        def block(b, carry):
            base = pl.multiple_of(b * 16, 16)
            tokens = pl.ds(base, 16)
            result = []
            for j in range(parts):
                lanes = slice(g * span + j * 128, g * span + (j + 1) * 128)
                delta = delta_ref[tokens, lanes]
                value = conv_ref[tokens, lanes]
                rate = -rate_ref[:, lanes]
                state = carry[j]
                rows = []
                for i in range(16):
                    retain = jnp.exp(delta[i : i + 1] * rate)
                    goal = in_ref[base + i] * value[i : i + 1]
                    state = goal + retain * (state - goal)
                    if emit:
                        rows.append(jnp.sum(out_coef_ref[base + i] * state, axis=0, keepdims=True))
                result.append(state)
                if emit:
                    scan_out = jnp.concatenate(rows, axis=0)
                    gate = gate_ref[tokens, lanes].astype(jnp.float32)
                    mixed = (scan_out + skip_ref[:, lanes] * value) * jax.nn.silu(gate)
                    out_ref[tokens, lanes] = mixed.astype(jnp.bfloat16)
            return tuple(result)

        return lax.fori_loop(0, blocks, block, begin)

    for g in range(groups):
        last = walk(g, (jnp.zeros((states, 128), jnp.float32),) * parts, False)
        for j in range(parts):
            own_end[g, :, j * 128 : (j + 1) * 128] = last[j].astype(jnp.bfloat16)
        own_sum[g] = jnp.sum(delta_ref[:, g * span : (g + 1) * span], axis=0, keepdims=True)
        if g == 0:
            pl.semaphore_wait(barrier, n - 1)
        for d in range(1, n):

            @pl.when(me + d < n)
            def _():
                for copy in copies(g, d):
                    copy.start()

    for g in range(groups):
        start[...] = jnp.zeros_like(start)
        for d in range(n - 1, 0, -1):

            @pl.when(me - d >= 0)
            def _():
                for copy in copies(g, d):
                    copy.wait_recv()
                decay = jnp.exp(-sums[g, d - 1] * rate_ref[:, g * span : (g + 1) * span])
                start[...] = decay * start[...] + ends[g, d - 1].astype(jnp.float32)

        walk(g, tuple(start[:, j * 128 : (j + 1) * 128] for j in range(parts)), True)

    for g in range(groups):
        for d in range(1, n):

            @pl.when(me + d < n)
            def _():
                for copy in copies(g, d):
                    copy.wait_send()


def mix(n, convolved, delta, input_coef, output_coef, decay_rate, skip_gain, gate_input):
    states, width = decay_rate.shape
    length = convolved.shape[0]
    span = 512
    groups = width // span
    vmem = pl.BlockSpec(memory_space=pltpu.VMEM)
    sems = pltpu.SemaphoreType.DMA((groups, n - 1))

    def spread(coef):
        return jnp.broadcast_to(coef.astype(jnp.float32)[:, :, None], (length, states, 128))

    return pl.pallas_call(
        functools.partial(mixer_kernel, n),
        out_shape=jax.ShapeDtypeStruct((length, width), jnp.bfloat16),
        in_specs=[vmem] * 7,
        out_specs=vmem,
        scratch_shapes=[
            pltpu.VMEM((groups, states, span), jnp.bfloat16),
            pltpu.VMEM((groups, 1, span), jnp.float32),
            pltpu.VMEM((groups, n - 1, states, span), jnp.bfloat16),
            pltpu.VMEM((groups, n - 1, 1, span), jnp.float32),
            pltpu.VMEM((states, span), jnp.float32),
            sems,
            sems,
            sems,
            sems,
        ],
        compiler_params=pltpu.CompilerParams(
            collective_id=0, has_side_effects=True, vmem_limit_bytes=VMEM_LIMIT
        ),
    )(
        convolved,
        delta,
        spread(input_coef),
        spread(output_coef),
        decay_rate,
        skip_gain[None, :],
        gate_input,
    )


def project_kernel(
    n, e, mixed_ref, weight_ref, out_ref, gath, part, zrecv, total, orecv,
    s_a, r_a, s_b, r_b, s_z, r_z, s_o, r_o,
):
    me, z, core, chip = place()
    nc = n // 2
    length, width = mixed_ref.shape
    cols = weight_ref.shape[1]
    rows = length // e
    partner = (me + 1 - 2 * core, z)
    greet(
        [(lax.rem(me + d, n), z) for d in range(1, n)]
        + [(me, lax.rem(z + d, e)) for d in range(1, e)]
    )

    across = []
    for d in range(1, nc):
        peer = (lax.rem(chip + d, nc) * 2 + core, z)
        across.append(push(mixed_ref, gath.at[me], s_a.at[d - 1], r_a.at[d - 1], peer))
        across[-1].start()
    beside = [push(mixed_ref, gath.at[me], s_b.at[0], r_b.at[0], partner)]
    beside[0].start()
    gath[me] = mixed_ref[...]

    along = []
    sent = []
    for d in range(nc):
        k = lax.rem(chip - d + nc, nc)
        if d + 1 < nc:
            across[d].wait_recv()
            src = lax.rem(chip - d - 1 + nc, nc) * 2 + core
            beside.append(push(gath.at[src], gath.at[src], s_b.at[d + 1], r_b.at[d + 1], partner))
            beside[-1].start()
        beside[d].wait_recv()
        block = gath[pl.ds(2 * k, 2)].reshape(2 * length, width)
        term = jnp.dot(block, weight_ref[...], preferred_element_type=jnp.float32)
        term = term.astype(jnp.bfloat16)
        for c in range(2):
            for q in range(e):
                begin = (c * e + q) * rows
                part[q, 2 * k + c] = term[begin : begin + rows]
        group = []
        for dz in range(1, e):
            q = lax.rem(z + dz, e)
            pair = pl.ds(2 * k, 2)
            group.append(
                push(part.at[q, pair], zrecv.at[z, pair], s_z.at[d, dz - 1], r_z.at[d, dz - 1], (me, q))
            )
            group[-1].start()
        along.append(group)

    for d in range(nc):
        k = lax.rem(chip - d + nc, nc)
        pair = pl.ds(2 * k, 2)
        acc = part[z, pair].astype(jnp.float32)
        for dz in range(1, e):
            along[d][dz - 1].wait_recv()
            acc = acc + zrecv[lax.rem(z - dz + e, e), pair].astype(jnp.float32)
        total[pair] = acc.astype(jnp.bfloat16)
        for c in ((0, 1) if d else (1,)):
            other = lax.rem(core + c, 2)
            s = 2 * k + other
            gap = lax.rem(me - s + n, n) - 1
            sent.append(push(total.at[s], orecv.at[me], s_o.at[gap], r_o.at[gap], (s, z)))
            sent[-1].start()
    orecv[me] = total[me]
    for g in range(n - 1):
        push(total.at[0], orecv.at[0], s_o.at[g], r_o.at[g], partner).wait_recv()
    for j in range(n):
        out_ref[:, j * cols : (j + 1) * cols] = orecv[j].astype(jnp.float32)
    for copy in across + beside + sum(along, []) + sent:
        copy.wait_send()


def project(n, e, mixed, out_weight):
    length, width = mixed.shape
    cols = out_weight.shape[1]
    rows = length // e
    vmem = pl.BlockSpec(memory_space=pltpu.VMEM)
    dma = pltpu.SemaphoreType.DMA
    nc = n // 2
    return pl.pallas_call(
        functools.partial(project_kernel, n, e),
        out_shape=jax.ShapeDtypeStruct((rows, n * cols), jnp.float32),
        in_specs=[vmem] * 2,
        out_specs=vmem,
        scratch_shapes=[
            pltpu.VMEM((n, length, width), jnp.bfloat16),
            pltpu.VMEM((e, n, rows, cols), jnp.bfloat16),
            pltpu.VMEM((e, n, rows, cols), jnp.bfloat16),
            pltpu.VMEM((n, rows, cols), jnp.bfloat16),
            pltpu.VMEM((n, rows, cols), jnp.bfloat16),
            dma((nc - 1,)),
            dma((nc - 1,)),
            dma((nc,)),
            dma((nc,)),
            dma((nc, e - 1)),
            dma((nc, e - 1)),
            dma((n - 1,)),
            dma((n - 1,)),
        ],
        compiler_params=pltpu.CompilerParams(
            collective_id=1, has_side_effects=True, vmem_limit_bytes=VMEM_LIMIT
        ),
        cost_estimate=pl.CostEstimate(
            flops=2 * n * length * width * cols, bytes_accessed=2 * width * cols, transcendentals=0
        ),
    )(mixed, out_weight)


def expert_kernel(
    n, e, tile, chunk,
    og_ref, pack_ref, unpack_ref, gate_hbm, up_hbm, down_hbm, out_ref,
    gate, up, down, disp, xs, act, ysend, yrecv, red, rbuf, ret, home,
    s_w, s_d, r_d, s_a, r_a, s_b, r_b, s_y, r_y, s_r, r_r, s_h, r_h,
):
    me, z, core, chip = place()
    nc = n // 2
    half = xs.shape[3]
    slots = xs.shape[2]
    hidden = act.shape[1]
    depth = 2 * half
    capp = og_ref.shape[1]
    other = 1 - core
    mate = me + 1 - 2 * core
    partner = (mate, z)

    loads = [
        pltpu.make_async_copy(gate_hbm.at[0], gate, s_w.at[0]),
        pltpu.make_async_copy(up_hbm.at[0], up, s_w.at[1]),
        pltpu.make_async_copy(down_hbm.at[0], down, s_w.at[2]),
    ]
    for load in loads:
        load.start()

    greet(
        [partner]
        + [(lax.rem(chip + d, nc) * 2 + core, z) for d in range(1, nc)]
        + [(s, lax.rem(z + d, e)) for d in range(1, e) for s in (me, mate)]
    )

    chunks = half // chunk

    def lanes(which, i):
        return pl.ds(pl.multiple_of(which * half + i * chunk, 128), chunk)

    routed = []
    for p in range(chunks):
        group = []
        for dz in range(e):
            q = lax.rem(z + dz, e)
            for dc in range(2):
                if dz == 0 and dc == 0:
                    continue
                s, c = ((me, core), (mate, other))[dc]
                i = 2 * dz + dc - 1
                src = og_ref.at[q, :, lanes(c, p)]
                group.append(push(src, disp.at[p, z, core], s_d.at[p, i], r_d.at[p, i], (s, q)))
                group[-1].start()
        disp[p, z, core] = og_ref[z, :, lanes(core, p)]
        routed.append(group)

    across = []
    beside = []

    def relay(p):
        for d in range(1, nc):
            across[p][d - 1].wait_recv()
            src = xs.at[lax.rem(chip - d + nc, nc), core, :, p * chunk : (p + 1) * chunk]
            beside[p].append(push(src, src, s_b.at[p, d], r_b.at[p, d], partner))
            beside[p][-1].start()

    for p in range(chunks):
        for copy in routed[p]:
            copy.wait_recv()
        xs[chip, core, :, p * chunk : (p + 1) * chunk] = jnp.dot(
            pack_ref[...], disp[p].reshape(2 * e * capp, chunk), preferred_element_type=jnp.float32
        ).astype(jnp.bfloat16)
        mine = xs.at[chip, core, :, p * chunk : (p + 1) * chunk]
        group = []
        for d in range(1, nc):
            peer = (lax.rem(chip + d, nc) * 2 + core, z)
            group.append(push(mine, mine, s_a.at[p, d - 1], r_a.at[p, d - 1], peer))
            group[-1].start()
        across.append(group)
        beside.append([push(mine, mine, s_b.at[p, 0], r_b.at[p, 0], partner)])
        beside[p][0].start()
        if p:
            relay(p - 1)
    relay(chunks - 1)
    for copy in sum(beside, []):
        copy.wait_recv()
    loads[0].wait()
    loads[1].wait()

    def up_step(f, carry):
        at = pl.ds(pl.multiple_of(f * tile, 128), tile)
        x0 = xs[:, 0].reshape(nc * slots, half)
        x1 = xs[:, 1].reshape(nc * slots, half)
        g = jnp.dot(x0, gate[0:half, at], preferred_element_type=jnp.float32)
        g = g + jnp.dot(x1, gate[half:depth, at], preferred_element_type=jnp.float32)
        u = jnp.dot(x0, up[0:half, at], preferred_element_type=jnp.float32)
        u = u + jnp.dot(x1, up[half:depth, at], preferred_element_type=jnp.float32)
        act[:, at] = (jax.nn.silu(g) * u).astype(jnp.bfloat16)
        return carry

    lax.fori_loop(0, hidden // tile, up_step, 0)
    loads[2].wait()

    def down_chunk(which, i):
        at = pl.ds(pl.multiple_of(which * half + i * chunk, 128), chunk)
        return jnp.dot(act[...], down[:, at], preferred_element_type=jnp.float32)

    paired = []
    for i in range(chunks):
        ysend[i] = down_chunk(other, i).astype(jnp.bfloat16)
        paired.append(push(ysend.at[i], yrecv.at[i], s_y.at[i], r_y.at[i], partner))
        paired[-1].start()
    summed = []
    back = []

    def settle(i):
        acc = red[i, chip].astype(jnp.float32)
        for d in range(1, nc):
            summed[i][d - 1].wait_recv()
            acc = acc + rbuf[i, d - 1].astype(jnp.float32)
        spread = jnp.dot(
            unpack_ref[...], acc.astype(jnp.bfloat16), preferred_element_type=jnp.float32
        ).astype(jnp.bfloat16)
        ret[i] = spread.reshape(e, 2, capp, chunk)
        for dz in range(e):
            q = lax.rem(z + dz, e)
            for dc in range(2):
                if dz == 0 and dc == 0:
                    continue
                s, c = ((me, core), (mate, other))[dc]
                k = 2 * dz + dc - 1
                dst = home.at[z, :, lanes(core, i)]
                back.append(push(ret.at[i, q, c], dst, s_h.at[i, k], r_h.at[i, k], (s, q)))
                back[-1].start()
        home[z, :, lanes(core, i)] = ret[i, z, core]

    for i in range(chunks):
        y = down_chunk(core, i)
        paired[i].wait_recv()
        y = (y + yrecv[i].astype(jnp.float32)).astype(jnp.bfloat16)
        red[i] = y.reshape(nc, slots, chunk)
        group = []
        for d in range(1, nc):
            k = lax.rem(chip + d, nc)
            group.append(
                push(red.at[i, k], rbuf.at[i, d - 1], s_r.at[i, d - 1], r_r.at[i, d - 1], (k * 2 + core, z))
            )
            group[-1].start()
        summed.append(group)
    for i in range(chunks):
        settle(i)

    for copy in back:
        copy.wait_recv()
    out_ref[...] = home[...]
    for copy in sum(routed + across + beside + summed, []) + paired + back:
        copy.wait_send()


def experts_apply(n, e, cap, outgoing, gate_weight, up_weight, down_weight):
    capp, width = outgoing.shape[1:]
    hidden = gate_weight.shape[2]
    nc = n // 2
    half = width // 2
    used = 2 * e * cap
    slots = -(-used // 16) * 16
    tile = 256 if hidden % 256 == 0 else 128
    chunk = 512
    chunks = half // chunk
    spots = jnp.arange(2 * e * capp)
    inside = spots % capp
    goal = jnp.where(inside < cap, (spots // capp) * cap + inside, -1)
    pack = (jnp.arange(slots)[:, None] == goal[None, :]).astype(jnp.bfloat16)
    vmem = pl.BlockSpec(memory_space=pltpu.VMEM)
    hbm = pl.BlockSpec(memory_space=pl.ANY)
    dma = pltpu.SemaphoreType.DMA
    bf = jnp.bfloat16
    return pl.pallas_call(
        functools.partial(expert_kernel, n, e, tile, chunk),
        out_shape=jax.ShapeDtypeStruct((e, capp, width), bf),
        in_specs=[vmem] * 3 + [hbm] * 3,
        out_specs=vmem,
        scratch_shapes=[
            pltpu.VMEM((width, hidden), bf),
            pltpu.VMEM((width, hidden), bf),
            pltpu.VMEM((hidden, width), bf),
            pltpu.VMEM((chunks, e, 2, capp, chunk), bf),
            pltpu.VMEM((nc, 2, slots, half), bf),
            pltpu.VMEM((nc * slots, hidden), bf),
            pltpu.VMEM((chunks, nc * slots, chunk), bf),
            pltpu.VMEM((chunks, nc * slots, chunk), bf),
            pltpu.VMEM((chunks, nc, slots, chunk), bf),
            pltpu.VMEM((chunks, nc - 1, slots, chunk), bf),
            pltpu.VMEM((chunks, e, 2, capp, chunk), bf),
            pltpu.VMEM((e, capp, width), bf),
            dma((3,)),
            dma((chunks, 2 * e - 1)),
            dma((chunks, 2 * e - 1)),
            dma((chunks, nc - 1)),
            dma((chunks, nc - 1)),
            dma((chunks, nc)),
            dma((chunks, nc)),
            dma((chunks,)),
            dma((chunks,)),
            dma((chunks, nc - 1)),
            dma((chunks, nc - 1)),
            dma((chunks, 2 * e - 1)),
            dma((chunks, 2 * e - 1)),
        ],
        compiler_params=pltpu.CompilerParams(
            collective_id=2, has_side_effects=True, vmem_limit_bytes=VMEM_LIMIT
        ),
        cost_estimate=pl.CostEstimate(
            flops=6 * nc * slots * width * hidden,
            bytes_accessed=6 * width * hidden,
            transcendentals=nc * slots * hidden,
        ),
    )(outgoing, pack, pack.T, gate_weight, up_weight, down_weight)


def shards(
    n,
    e,
    mixer_input,
    gate_input,
    delta_raw,
    input_coef,
    output_coef,
    decay_rate,
    conv_weight,
    conv_bias,
    skip_gain,
    out_weight,
    residual,
    norm_gain,
    router_weight,
    expert_ids,
    gate_weight,
    up_weight,
    down_weight,
):
    length = mixer_input.shape[0]
    width = mixer_input.shape[1]
    tail = mixer_input[length - (KCONV - 1) :]
    before = from_behind(tail, "seq", 1)
    padded = jnp.concatenate([before, mixer_input], axis=0).astype(jnp.float32)
    summed = jnp.broadcast_to(conv_bias[None, :], (length, width))
    for offset in range(KCONV):
        summed = summed + conv_weight[offset][None, :] * padded[offset : offset + length]
    convolved = jax.nn.silu(summed)
    delta = jax.nn.softplus(delta_raw.astype(jnp.float32))
    mixed = mix(
        n, convolved, delta, input_coef, output_coef, decay_rate, skip_gain, gate_input
    )
    rows = residual.shape[0]
    model_width = residual.shape[1]
    projected = project(n, e, mixed, out_weight)
    hidden_state = residual.astype(jnp.float32) + projected
    scale = lax.rsqrt(jnp.mean(hidden_state * hidden_state, axis=1, keepdims=True) + 1e-06)
    normed = (hidden_state * scale * norm_gain[None, :]).astype(jnp.bfloat16)
    capacity = 2 * rows // e + 1
    capp = -(-capacity // 16) * 16
    logits = jnp.dot(normed, router_weight, preferred_element_type=jnp.float32)
    expert_range = jnp.arange(e, dtype=jnp.int32)
    matches = expert_ids[:, :, None] == expert_range[None, None, :]
    chosen = jnp.sum(jnp.where(matches, logits[:, None, :], 0.0), axis=2)
    first = jax.nn.sigmoid(chosen[:, 0] - chosen[:, 1])
    flat_ids = expert_ids.reshape(-1)
    onehot = (flat_ids[:, None] == expert_range[None, :]).astype(jnp.int32)
    rank = jnp.sum((jnp.cumsum(onehot, axis=0) - onehot) * onehot, axis=1)
    target = flat_ids * capp + rank
    slot_range = jnp.arange(e * capp, dtype=jnp.int32)
    placing = (slot_range[:, None, None] == target.reshape(rows, 2)[None]).astype(jnp.bfloat16)
    outgoing = (
        jnp.dot(placing[:, :, 0] + placing[:, :, 1], normed, preferred_element_type=jnp.float32)
        .astype(jnp.bfloat16)
        .reshape(e, capp, model_width)
    )
    returned = experts_apply(n, e, capacity, outgoing, gate_weight, up_weight, down_weight)
    flat_returned = returned.reshape(-1, model_width)
    picked = [
        jnp.einsum("sa,sd->ad", placing[:, :, k], flat_returned, preferred_element_type=jnp.float32)
        for k in range(2)
    ]
    moe_out = first[:, None] * picked[0] + (1.0 - first)[:, None] * picked[1]
    final = (hidden_state + moe_out).astype(jnp.bfloat16)
    return (mixed, final)


def solution(mesh):
    return jax.shard_map(
        functools.partial(shards, mesh.shape["seq"], mesh.shape["exp"]),
        mesh=mesh,
        in_specs=(
            P("seq", "exp"),
            P("seq", "exp"),
            P("seq", "exp"),
            P("seq", None),
            P("seq", None),
            P(None, "exp"),
            P(None, "exp"),
            P("exp"),
            P("exp"),
            P("exp", "seq"),
            P(("seq", "exp"), None),
            P(),
            P(),
            P(("seq", "exp"), None),
            P("exp", None, "seq"),
            P("exp", None, "seq"),
            P("exp", "seq", None),
        ),
        out_specs=(P("seq", "exp"), P(("seq", "exp"), None)),
        check_vma=False,
    )
```
